256 devices in a mesh: seg: 8 (over x, core), sec: 32 (over z, y).
Axes of the slice: x: 4, y: 4, z: 8, core: 2. Of those that a mesh axis runs over, the one named last changes fastest.
Arguments:
- environment: bfloat16 [8, 256, 17, 128, 128], P('seg', 'sec'), may hold values from -0.25 to 0.25
- block_energy: bfloat16 [8, 256, 128], P('seg', 'sec'), may hold values from 0 to 10
- basis_dims: int32 [8, 256], P('seg', 'sec'), may hold values from 42 to 128, as said below
- start_wave: bfloat16 [8, 256, 128, 128], P('seg', 'sec'), may hold values from -16 to 16
Outputs:
- wave: bfloat16 [8, 256, 128, 128], P('seg', 'sec')
The draws below stay inside these ranges and needn't reach their ends.
Inputs may be any that keep to these rules, and one draw needn't show every extreme that they name: `basis_dims`: in every segment one sector keeps 128 states and another a third of 128, rounded down.
All inputs are finite; a program needn't handle non-finite values.
Results may differ from the reference program's by a relative error of at most 0.0085.
Values may be sent and summed in bfloat16 or wider, within the bound.
A program may use at most 128 MiB of HBM per device.

```python
import jax
import jax.numpy as jnp
from jax import lax

BS = 128
W = 17
ITERS = 4
BONDS = 8
NB = 256


def draw_block_energy(key, part):
    key = jax.random.fold_in(key, 3)
    sector = jnp.arange(NB, dtype=jnp.float32)[None, :, None] / (NB - 1)
    base = jax.random.uniform(key, (BONDS, NB, BS), jnp.float32, 0.0, 4.0)
    value = base + 4.0 * sector
    return value.astype(jnp.bfloat16)


def draw_basis_dims(key, part):
    key = jax.random.fold_in(key, 7)
    keys = jax.random.split(key, 3)
    kept = jax.random.randint(keys[0], (BONDS, NB), BS // 3, BS + 1, dtype=jnp.int32)
    full_at = jax.random.randint(keys[1], (BONDS, 1), 0, NB, dtype=jnp.int32)
    offset = jax.random.randint(keys[2], (BONDS, 1), 1, NB, dtype=jnp.int32)
    least_at = (full_at + offset) % NB
    column = jnp.arange(NB, dtype=jnp.int32)[None, :]
    kept = jnp.where(column == full_at, BS, kept)
    kept = jnp.where(column == least_at, BS // 3, kept)
    return kept.astype(jnp.int32)


def draw_start_wave(key, part):
    key = jax.random.fold_in(key, 5)
    sector = jnp.arange(NB, dtype=jnp.float32)[None, :, None, None] / (NB - 1)
    base = jnp.clip(jax.random.normal(key, (BONDS, NB, BS, BS), jnp.float32), -4.0, 4.0)
    value = base * (1.0 + 2.0 * sector)
    return value.astype(jnp.bfloat16)


def level_of(own_key, shape, shards, least, largest):
    loudness = 1.0
    for dim, blocks in shards:
        draws = jax.random.uniform(jax.random.fold_in(jax.random.fold_in(own_key, 6), dim), (blocks,), jnp.float32, least / len(shards), largest / len(shards))
        loudness = loudness * jnp.repeat(jnp.exp(draws), shape[dim] // blocks).reshape((-1,) + (1,) * (len(shape) - 1 - dim))
    return loudness


def noise(stream_key, shape, scale, bound, cuts=(), kind=jnp.bfloat16):
    gain = level_of(stream_key, shape, cuts, -0.22, 0.18) if cuts else 1.0
    drawn = jax.random.normal(stream_key, shape, jnp.float32) * scale * gain
    return jnp.minimum(jnp.maximum(drawn, -bound), bound).astype(kind)


def setup_inputs(seed: int = 0) -> dict:
    streams_of = jax.random.split(jax.random.key(seed), 5)
    return {
        "environment": noise(streams_of[0], (BONDS, NB, W, BS, BS), (4 * BS) ** -0.5, 0.25, ((0, 8), (1, 32))),
        "block_energy": draw_block_energy(jax.random.fold_in(streams_of[4], 71), 0),
        "basis_dims": draw_basis_dims(jax.random.fold_in(streams_of[4], 71), 0),
        "start_wave": draw_start_wave(jax.random.fold_in(streams_of[4], 71), 0),
    }


norm_floor = 1e-06

def rounded(value):
    return lax.optimization_barrier(value.astype(jnp.bfloat16)).astype(jnp.float32)

def symmetric_env(env):
    widened = env.astype(jnp.float32)
    return rounded(widened + jnp.swapaxes(widened, -1, -2))

def operate(left_sym, right_sym, diag_energy, mask, vector):
    vec_half = rounded(vector)
    right_part = rounded(jnp.einsum('sij,swjk->swik', vec_half, right_sym, precision=lax.Precision.HIGHEST))
    total = jnp.einsum('swij,swjk->sik', left_sym, right_part, precision=lax.Precision.HIGHEST)
    return mask * (total + diag_energy * vector)

def rotation(rayleigh, coupling, curvature):
    half_gap = 0.5 * (rayleigh - curvature)
    radius = jnp.sqrt(half_gap * half_gap + coupling * coupling)
    ritz = 0.5 * (rayleigh + curvature) - radius
    first = coupling + curvature - ritz
    second = -(coupling + rayleigh - ritz)
    length = jnp.sqrt(first * first + second * second)
    return (first / length, second / length)

def reference(environment, block_energy, basis_dims, start_wave):
    count = float(NB * BS * BS)

    def inner(left_field, right_field):
        return jnp.sum(left_field * right_field) / count

    def one_bond(bond):
        after = (bond + 1) % BONDS
        left_sym = symmetric_env(environment[bond])
        right_sym = symmetric_env(environment[after])
        left_energy = block_energy[bond].astype(jnp.float32)
        right_energy = block_energy[after].astype(jnp.float32)
        rows_kept = basis_dims[bond].astype(jnp.float32)
        cols_kept = basis_dims[after].astype(jnp.float32)
        position = jnp.arange(BS, dtype=jnp.float32)[None, :]
        row_live = (position < rows_kept[:, None]).astype(jnp.float32)
        col_live = (position < cols_kept[:, None]).astype(jnp.float32)
        mask = row_live[:, :, None] * col_live[:, None, :]
        diag_energy = left_energy[:, :, None] + right_energy[:, None, :]
        left_diag = jnp.diagonal(left_sym, axis1=2, axis2=3)
        right_diag = jnp.diagonal(right_sym, axis1=2, axis2=3)
        diag_full = jnp.einsum('swi,swj->sij', left_diag, right_diag, precision=lax.Precision.HIGHEST) + diag_energy
        vector = mask * start_wave[bond].astype(jnp.float32)
        vector = vector / jnp.sqrt(inner(vector, vector) + norm_floor)
        image = operate(left_sym, right_sym, diag_energy, mask, vector)
        for step in range(ITERS):
            rayleigh = inner(vector, image)
            trial = mask * (image - rayleigh * vector) / jnp.maximum(jnp.abs(diag_full - rayleigh), 1.0)
            correlation = inner(vector, trial)
            trial = trial - correlation * vector
            trial = trial / jnp.sqrt(inner(trial, trial) + norm_floor)
            trial_image = operate(left_sym, right_sym, diag_energy, mask, trial)
            coupling = inner(trial, image)
            curvature = inner(trial, trial_image)
            cosine, sine = rotation(rayleigh, coupling, curvature)
            vector = cosine * vector + sine * trial
            image = cosine * image + sine * trial_image
        return vector.astype(jnp.bfloat16)
    return lax.map(one_bond, jnp.arange(BONDS, dtype=jnp.int32))
```

```python
import functools

import jax
import jax.numpy as jnp
from jax import lax
from jax.experimental import pallas as pl
from jax.experimental.pallas import tpu as pltpu
from jax.sharding import PartitionSpec as P

ITERS = 4
SEG, SEC, YS, ZS = 8, 32, 4, 8
NS, W, BS = 8, 17, 128
WP = 32
PAIRS = 4
SPLITS = ((0, 9), (9, 17))
NORM_FLOOR = 1e-06
COUNT = float(SEC * NS * BS * BS)
MESH = pl.DeviceIdType.MESH
f32, bf16 = jnp.float32, jnp.bfloat16


def hops(offset):
    a, b, c = offset
    return abs(a) + min(b, YS - b) + min(c, ZS - c)


PEERS = [
    (a, b, c)
    for a in (-1, 0, 1)
    for b in range(YS)
    for c in range(ZS)
    if (a, b, c) != (0, 0, 0)
]
FAR_FIRST = sorted(PEERS, key=lambda o: -hops(o))
ROW = {}
for a_, base_ in ((1, 0), (-1, SEC), (0, 2 * SEC)):
    for i_, o_ in enumerate([o for o in PEERS if o[0] == a_]):
        ROW[o_] = base_ + i_


def fold(product):
    return jnp.sum(product.reshape(BS // 8, 8, BS), axis=0)


def rotation(rayleigh, coupling, curvature):
    half_gap = 0.5 * (rayleigh - curvature)
    radius = jnp.sqrt(half_gap * half_gap + coupling * coupling)
    ritz = 0.5 * (rayleigh + curvature) - radius
    first = coupling + curvature - ritz
    second = -(coupling + rayleigh - ritz)
    length = jnp.sqrt(first * first + second * second)
    return first / length, second / length


def kernel(
    dims_ref, energy_ref, env_ref, start_ref, out_ref,
    env, packed, arrived, diag_f, diag, far_diag_f, own_start, far_start,
    meta_out, meta_in, meta, vec, img, tri, tri_img, diag_full, energy, mask,
    part, rows, coef, far_tri, far_vec,
    env_sem, start_sem, meta_s, meta_r, start_s, start_r, diag_s, diag_r,
    pack_s, pack_r, tri_s, tri_r, red_s, red_r,
):
    k = lax.axis_index("seg")
    s = lax.axis_index("sec")
    z, y = lax.div(s, YS), lax.rem(s, YS)
    core = lax.rem(k, 2)
    seg_of = {a: lax.rem(k + a + SEG, SEG) for a in (-1, 0, 1)}
    y_of = [lax.rem(y + b, YS) for b in range(YS)]
    z_of = [lax.rem(z + c, ZS) * YS for c in range(ZS)]

    def peer(o):
        return (seg_of[o[0]], z_of[o[2]] + y_of[o[1]])

    before, after = (seg_of[-1], s), (seg_of[1], s)

    slow_out = 2 * core
    slow_in = 2 - 2 * core
    out_order = (slow_out, slow_out + 1, slow_in, slow_in + 1)
    in_order = (slow_out, slow_out + 1, slow_in, slow_in + 1)

    def env_copy(i):
        p = out_order[i]
        return pltpu.make_async_copy(
            env_ref.at[pl.ds(2 * p, 2)], env.at[pl.ds(2 * p, 2)], env_sem.at[i]
        )

    for i in range(PAIRS):
        env_copy(i).start()
    own_start_copy = pltpu.make_async_copy(start_ref, own_start, start_sem)
    own_start_copy.start()

    barrier = pltpu.get_barrier_semaphore()
    for o in FAR_FIRST:
        pl.semaphore_signal(barrier, inc=1, device_id=peer(o), device_id_type=MESH)

    kept = jnp.concatenate(
        [jnp.full((1, BS), dims_ref[0, j].astype(f32), f32) for j in range(NS)], axis=0
    )
    own_meta = jnp.concatenate([energy_ref[...].astype(f32), kept], axis=0)
    meta_out[...] = own_meta.astype(bf16)
    meta[0] = own_meta

    row = lax.broadcasted_iota(jnp.int32, (BS, BS), 0)
    col = lax.broadcasted_iota(jnp.int32, (BS, BS), 1)
    upper = row <= col
    on_diag = row == col

    diag_f[...] = jnp.zeros_like(diag_f)
    far_tri[0] = jnp.zeros((NS // 2, BS, BS), f32)
    tri[...] = jnp.zeros_like(tri)
    tri_img[...] = jnp.zeros_like(tri_img)

    def symmetrise(p, w, _):
        halves = []
        for q in range(2):
            u = 2 * p + q
            raw = env[u, w]
            whole = raw.astype(f32) + jnp.swapaxes(raw, 0, 1).astype(f32)
            env[u, w] = whole.astype(bf16)
            halves.append(whole)
            diag_f[u, pl.ds(w, 1), :] = jnp.sum(
                jnp.where(on_diag, whole, 0.0), axis=0, keepdims=True
            )
        packed[p, w] = jnp.where(upper, halves[0], halves[1]).astype(bf16)
        return 0

    def pack_copy(p, c):
        lo, hi = SPLITS[c]
        target = jnp.where(p < 2, before[0], after[0])
        return pltpu.make_async_remote_copy(
            src_ref=packed.at[p, pl.ds(lo, hi - lo)],
            dst_ref=arrived.at[p, pl.ds(lo, hi - lo)],
            send_sem=pack_s.at[p, c], recv_sem=pack_r.at[p, c],
            device_id=(target, s), device_id_type=MESH,
        )

    def diag_copy(p):
        target = jnp.where(p < 2, before[0], after[0])
        return pltpu.make_async_remote_copy(
            src_ref=diag.at[pl.ds(2 * p, 2)], dst_ref=diag.at[pl.ds(NS + 2 * p, 2)],
            send_sem=diag_s.at[p], recv_sem=diag_r.at[p],
            device_id=(target, s), device_id_type=MESH,
        )

    meta_copies = [
        pltpu.make_async_remote_copy(
            src_ref=meta_out, dst_ref=meta_in.at[slot],
            send_sem=meta_s.at[slot], recv_sem=meta_r.at[slot],
            device_id=target, device_id_type=MESH,
        )
        for slot, target in ((0, before), (1, after))
    ]
    start_copy = pltpu.make_async_remote_copy(
        src_ref=start_ref.at[pl.ds(NS // 2, NS // 2)], dst_ref=far_start,
        send_sem=start_s, recv_sem=start_r, device_id=after, device_id_type=MESH,
    )

    for i in range(PAIRS):
        p = out_order[i]
        env_copy(i).wait()
        for c, (lo, hi) in enumerate(SPLITS):
            lax.fori_loop(lo, hi, functools.partial(symmetrise, p), 0)
            if i == 0 and c == 0:
                pl.semaphore_wait(barrier, len(PEERS))
                for copy in meta_copies:
                    copy.start()
                start_copy.start()
            if c == len(SPLITS) - 1:
                for q in range(2):
                    diag[2 * p + q] = diag_f[2 * p + q].astype(bf16)
                diag_copy(p).start()
            pack_copy(p, c).start()

    own_start_copy.wait()
    for slot, copy in enumerate(meta_copies):
        copy.wait()
        meta[1 + slot] = meta_in[slot].astype(f32)
    start_copy.wait()

    def left_at(u):
        return jnp.where(u < 4, u, NS + u)

    def right_at(u):
        return jnp.where(u < 4, NS + u, u)

    def mask_of(row_seg, col_seg, u):
        rows_kept = meta[row_seg, pl.ds(NS + u, 1), :]
        cols_kept = meta[col_seg, pl.ds(NS + u, 1), :]
        live = (row.astype(f32) < rows_kept) & (col.astype(f32) < cols_kept)
        return live.astype(f32)

    def set_up(u, _):
        row_seg = jnp.where(u < 4, 0, 2)
        col_seg = jnp.where(u < 4, 1, 0)
        live = mask_of(row_seg, col_seg, u)
        mask[u] = live
        by_row = jnp.broadcast_to(meta[row_seg, pl.ds(u, 1), :], (BS, BS))
        energy[u] = jnp.swapaxes(by_row, 0, 1) + meta[col_seg, pl.ds(u, 1), :]
        return 0

    lax.fori_loop(0, NS, set_up, 0)
    for j in range(NS // 2):
        vec[j] = mask[j] * own_start[j].astype(f32)
        vec[4 + j] = mask[4 + j] * far_start[j].astype(f32)
        far_vec[j] = mask_of(0, 1, 4 + j) * own_start[4 + j].astype(f32)

    def apply_env(x, u, lo, hi):
        n = hi - lo
        left = env[left_at(u), pl.ds(lo, n)].reshape(n * BS, BS)
        right = env[right_at(u), pl.ds(lo, n)].reshape(n * BS, BS)
        half = jnp.dot(left, x, preferred_element_type=f32).astype(bf16)
        half = half.reshape(n, BS, BS)
        half = jnp.concatenate([half[w] for w in range(n)], axis=1)
        return jnp.dot(half, right, preferred_element_type=f32)

    def unpack(p, w, _):
        sent = arrived[p, w]
        there = sent.astype(f32)
        back = jnp.swapaxes(sent, 0, 1).astype(f32)
        u = NS + 2 * p
        env[u, w] = jnp.where(upper, there, back).astype(bf16)
        second = jnp.where(upper, back, there)
        second = jnp.where(on_diag, far_diag_f[p, pl.ds(w, 1), :], second)
        env[u + 1, w] = second.astype(bf16)
        return 0

    for i in range(PAIRS):
        p = in_order[i]
        for c, (lo, hi) in enumerate(SPLITS):
            if c == 0:
                diag_copy(p).wait_recv()
                far_diag_f[p] = diag[NS + 2 * p + 1].astype(f32)
            pack_copy(p, c).wait_recv()
            lax.fori_loop(lo, hi, functools.partial(unpack, p), 0)
            for q in range(2):
                u = 2 * p + q
                more = apply_env(vec[u].astype(bf16), u, lo, hi)
                if c == 0:
                    img[u] = more
                else:
                    img[u] = mask[u] * (img[u] + more + energy[u] * vec[u])
            if c == len(SPLITS) - 1:
                for q in range(2):
                    u = 2 * p + q
                    both = lax.dot_general(
                        diag[left_at(u)], diag[right_at(u)],
                        (((0,), (0,)), ((), ())), preferred_element_type=f32,
                    )
                    diag_full[u] = both + energy[u]

    lane = lax.broadcasted_iota(jnp.int32, (1, BS), 1)
    pick = lax.broadcasted_iota(jnp.int32, (16, BS), 0) == lax.broadcasted_iota(
        jnp.int32, (16, BS), 1
    )
    nothing = jnp.zeros((8, BS), f32)

    def send_sums(step, this_bond, bond_before):
        tile = [jnp.sum(x, axis=0, keepdims=True) for x in this_bond]
        tile += [jnp.zeros((8 - len(this_bond), BS), f32)]
        tile += [jnp.sum(x, axis=0, keepdims=True) for x in bond_before]
        tile += [jnp.zeros((8 - len(bond_before), BS), f32)]
        tile = jnp.sum(jnp.concatenate(tile, axis=0), axis=1, keepdims=True)
        line = jnp.sum(jnp.where(pick, tile, 0.0), axis=0, keepdims=True)
        part[step] = line
        for o in FAR_FIRST:
            pltpu.make_async_remote_copy(
                src_ref=part.at[step], dst_ref=rows.at[step, ROW[o]],
                send_sem=red_s.at[step], recv_sem=red_r.at[step],
                device_id=peer(o), device_id_type=MESH,
            ).start()

    def total_of(step):
        pltpu.make_async_copy(rows.at[step], rows.at[step], red_r.at[step]).wait()
        from_before = jnp.sum(rows[step, 0:SEC], axis=0)
        from_after = jnp.sum(rows[step, SEC : 2 * SEC], axis=0)
        here = jnp.sum(rows[step, 2 * SEC : 3 * SEC - 1], axis=0) + part[step]
        crossed = jnp.where(
            lane < 8, pltpu.roll(from_after, BS - 8, 1), pltpu.roll(from_before, 8, 1)
        )
        return (here + crossed) / COUNT

    def nth(total, q):
        return pltpu.roll(total, BS - q, 1) if q else total

    def keep_coefs(scale_vec, scale_tri, rayleigh):
        for b in range(2):
            for i, value in enumerate((scale_vec, scale_tri, rayleigh)):
                one = jnp.sum(
                    jnp.where(lane == 8 * b, value, 0.0), axis=1, keepdims=True
                )
                coef[b, pl.ds(i, 1), :] = jnp.broadcast_to(one, (1, BS))

    def first_sums(u, sums):
        x = vec[u]
        return (sums[0] + fold(x * x), sums[1] + fold(x * img[u]))

    sums_here = lax.fori_loop(0, 4, first_sums, (nothing, nothing))
    sums_before = lax.fori_loop(4, 8, first_sums, (nothing, nothing))
    send_sums(0, sums_here, sums_before)
    total = total_of(0)
    start_sq, energy_sum = nth(total, 0), nth(total, 1)
    scale = 1.0 / jnp.sqrt(start_sq + NORM_FLOOR)
    rayleigh = energy_sum * scale * scale
    vec_sq = start_sq * scale * scale
    keep_coefs(scale, jnp.zeros((1, BS), f32), rayleigh)

    def tri_copy(it, p):
        return pltpu.make_async_remote_copy(
            src_ref=tri.at[pl.ds(2 * p, 2)], dst_ref=far_tri.at[it + 1, pl.ds(2 * p - 4, 2)],
            send_sem=tri_s.at[it, p - 2], recv_sem=tri_r.at[it, p - 2],
            device_id=before, device_id_type=MESH,
        )

    def advance(u):
        b = jnp.where(u < 4, 0, 1)
        grow_vec, grow_tri = coef[b, pl.ds(0, 1), :], coef[b, pl.ds(1, 1), :]
        ray = coef[b, pl.ds(2, 1), :]
        x = grow_vec * vec[u] + grow_tri * tri[u]
        h = grow_vec * img[u] + grow_tri * tri_img[u]
        vec[u] = x
        img[u] = h
        t = (h - ray * x) / jnp.maximum(jnp.abs(diag_full[u] - ray), 1.0)
        tri[u] = t
        return t

    def measure(u, t, sums):
        th = mask[u] * (apply_env(t.astype(bf16), u, 0, W) + energy[u] * t)
        tri_img[u] = th
        x, h = vec[u], img[u]
        return (
            sums[0] + fold(x * t), sums[1] + fold(t * t), sums[2] + fold(t * h),
            sums[3] + fold(t * th), sums[4] + fold(x * th),
        )

    def step_before(it, p, sums):
        trials = [advance(2 * p + q) for q in range(2)]
        tri_copy(it, p).start()
        for q in range(2):
            sums = measure(2 * p + q, trials[q], sums)
        return sums

    def step_here(p, sums):
        trials = [advance(2 * p + q) for q in range(2)]
        for q in range(2):
            sums = measure(2 * p + q, trials[q], sums)
        return sums

    def iteration(it, carried):
        rayleigh, vec_sq = carried
        sums_before = lax.fori_loop(2, 4, functools.partial(step_before, it), (nothing,) * 5)
        sums_here = lax.fori_loop(0, 2, step_here, (nothing,) * 5)
        send_sums(it + 1, sums_here, sums_before)

        @pl.when(it >= 1)
        def _():
            for p in (2, 3):
                tri_copy(it - 1, p).wait_recv()

        def follow(j, _):
            far_vec[j] = (
                coef[0, pl.ds(0, 1), :] * far_vec[j]
                + coef[0, pl.ds(1, 1), :] * far_tri[it, j]
            )
            return 0

        lax.fori_loop(0, NS // 2, follow, 0)

        total = total_of(it + 1)
        vt, tt, ti, th, vh = (nth(total, q) for q in range(5))
        trial_sq = jnp.maximum(tt - vt * vt * (2.0 - vec_sq), 0.0)
        shrink = 1.0 / jnp.sqrt(trial_sq + NORM_FLOOR)
        cross = vh + ti
        coupling = (ti - vt * rayleigh) * shrink
        curvature = (th - vt * cross + vt * vt * rayleigh) * shrink * shrink
        cosine, sine = rotation(rayleigh, coupling, curvature)
        grow_tri = sine * shrink
        grow_vec = cosine - grow_tri * vt
        mixed = grow_vec * grow_tri
        new_rayleigh = (
            grow_vec * grow_vec * rayleigh + mixed * cross + grow_tri * grow_tri * th
        )
        new_sq = grow_vec * grow_vec * vec_sq + 2.0 * mixed * vt + grow_tri * grow_tri * tt
        keep_coefs(grow_vec, grow_tri, new_rayleigh)
        for p in (2, 3):
            tri_copy(it, p).wait_send()
        return new_rayleigh, new_sq

    lax.fori_loop(0, ITERS, iteration, (rayleigh, vec_sq))

    grow_vec, grow_tri = coef[0, pl.ds(0, 1), :], coef[0, pl.ds(1, 1), :]
    for j in range(NS // 2):
        out_ref[j] = (grow_vec * vec[j] + grow_tri * tri[j]).astype(bf16)
    for p in (2, 3):
        tri_copy(ITERS - 1, p).wait_recv()
    for j in range(NS // 2):
        out_ref[4 + j] = (grow_vec * far_vec[j] + grow_tri * far_tri[ITERS, j]).astype(bf16)

    for i in range(PAIRS):
        diag_copy(out_order[i]).wait_send()
        for c in range(len(SPLITS)):
            pack_copy(out_order[i], c).wait_send()
    for step in range(ITERS + 1):
        pltpu.make_async_copy(rows.at[step], rows.at[step], red_s.at[step]).wait()


def per_device(environment, block_energy, basis_dims, start_wave):
    block = (NS, BS, BS)
    half = (NS // 2, BS, BS)
    dma = pltpu.SemaphoreType.DMA
    splits = len(SPLITS)
    wave = pl.pallas_call(
        kernel,
        out_shape=jax.ShapeDtypeStruct(block, bf16),
        in_specs=[
            pl.BlockSpec(memory_space=pltpu.SMEM),
            pl.BlockSpec(memory_space=pltpu.VMEM),
            pl.BlockSpec(memory_space=pl.ANY),
            pl.BlockSpec(memory_space=pl.ANY),
        ],
        out_specs=pl.BlockSpec(memory_space=pltpu.VMEM),
        scratch_shapes=[
            pltpu.VMEM((2 * NS, W, BS, BS), bf16),
            pltpu.VMEM((PAIRS, W, BS, BS), bf16),
            pltpu.VMEM((PAIRS, W, BS, BS), bf16),
            pltpu.VMEM((NS, WP, BS), f32),
            pltpu.VMEM((2 * NS, WP, BS), bf16),
            pltpu.VMEM((PAIRS, WP, BS), f32),
            pltpu.VMEM(block, bf16),
            pltpu.VMEM(half, bf16),
            pltpu.VMEM((16, BS), bf16),
            pltpu.VMEM((2, 16, BS), bf16),
            pltpu.VMEM((3, 16, BS), f32),
            pltpu.VMEM(block, f32),
            pltpu.VMEM(block, f32),
            pltpu.VMEM(block, f32),
            pltpu.VMEM(block, f32),
            pltpu.VMEM(block, f32),
            pltpu.VMEM(block, f32),
            pltpu.VMEM(block, f32),
            pltpu.VMEM((ITERS + 1, 1, BS), f32),
            pltpu.VMEM((ITERS + 1, len(PEERS), 1, BS), f32),
            pltpu.VMEM((2, 8, BS), f32),
            pltpu.VMEM((ITERS + 1,) + half, f32),
            pltpu.VMEM(half, f32),
            dma((PAIRS,)), dma, dma((2,)), dma((2,)), dma, dma,
            dma((PAIRS,)), dma((PAIRS,)),
            dma((PAIRS, splits)), dma((PAIRS, splits)),
            dma((ITERS, 2)), dma((ITERS, 2)),
            dma((ITERS + 1,)), dma((ITERS + 1,)),
        ],
        compiler_params=pltpu.CompilerParams(
            collective_id=0, has_side_effects=True, vmem_limit_bytes=48 * 2**20
        ),
    )(basis_dims, block_energy[0], environment[0], start_wave[0])
    return wave[None]


def solution(mesh):
    placed = (
        P("seg", "sec", None, None, None),
        P("seg", "sec", None),
        P("seg", "sec"),
        P("seg", "sec", None, None),
    )
    return jax.shard_map(
        per_device,
        mesh=mesh,
        in_specs=placed,
        out_specs=P("seg", "sec", None, None),
        check_vma=False,
    )
```

```python
import functools

import jax
import jax.numpy as jnp
from jax import lax
from jax.experimental import pallas as pl
from jax.experimental.pallas import tpu as pltpu
from jax.sharding import PartitionSpec as P

ITERS = 4
SEG, SEC, YS, ZS = 8, 32, 4, 8
NS, W, BS = 8, 17, 128
WP = 32
PAIRS = 4
SPLITS = ((0, 8), (8, 17))
GROUP = 4
NORM_FLOOR = 1e-06
COUNT = float(SEC * NS * BS * BS)
MESH = pl.DeviceIdType.MESH
f32, bf16 = jnp.float32, jnp.bfloat16


def hops(offset):
    a, b, c = offset
    return abs(a) + min(b, YS - b) + min(c, ZS - c)


PEERS = [
    (a, b, c)
    for a in (0, 1)
    for b in range(YS)
    for c in range(ZS)
    if (a, b, c) != (0, 0, 0)
]
X_SIDES, Y_SIDES, Z_SIDES = (
    ((-1, 0, 0), (1, 0, 0)),
    ((0, 1, 0), (0, YS - 1, 0)),
    ((0, 0, 1), (0, 0, ZS - 1)),
)
GOSSIP = (Z_SIDES, Z_SIDES, Z_SIDES, Y_SIDES, Y_SIDES, X_SIDES)
FAR_FIRST = sorted(PEERS, key=lambda o: -hops(o))
ROW = {}
for a_, base_ in ((1, 0), (0, SEC)):
    for i_, o_ in enumerate([o for o in PEERS if o[0] == a_]):
        ROW[o_] = base_ + i_


def fold(product):
    return jnp.sum(product.reshape(BS // 8, 8, BS), axis=0)


def rotation(rayleigh, coupling, curvature):
    half_gap = 0.5 * (rayleigh - curvature)
    radius = jnp.sqrt(half_gap * half_gap + coupling * coupling)
    ritz = 0.5 * (rayleigh + curvature) - radius
    first = coupling + curvature - ritz
    second = -(coupling + rayleigh - ritz)
    length = jnp.sqrt(first * first + second * second)
    return first / length, second / length


def kernel(
    dims_hbm, energy_hbm, env_ref, start_ref, out_ref,
    dims_ref, energy_ref, env, packed, arrived, diag_f, diag, far_diag_f, own_start, far_start,
    meta_out, meta_in, meta, vec, img, tri, tri_img, diag_full, energy, mask,
    part, rows, state, far_tri, far_vec,
    gossip, small_sem, env_sem, start_sem, meta_s, meta_r, start_s, start_r, diag_s, diag_r,
    pack_s, pack_r, tri_s, tri_r, red_s, red_r,
):
    k = lax.axis_index("seg")
    s = lax.axis_index("sec")
    z, y = lax.div(s, YS), lax.rem(s, YS)
    core = lax.rem(k, 2)
    seg_of = {a: lax.rem(k + a + SEG, SEG) for a in (-1, 0, 1)}
    y_of = [lax.rem(y + b, YS) for b in range(YS)]
    z_of = [lax.rem(z + c, ZS) * YS for c in range(ZS)]

    def peer(o):
        a, b, c = o
        return (seg_of[a], z_of[c] + y_of[b])

    before, after = (seg_of[-1], s), (seg_of[1], s)

    slow_out = 2 * core
    slow_in = 2 - 2 * core
    out_order = (slow_out, slow_out + 1, slow_in, slow_in + 1)
    in_order = (slow_out, slow_out + 1, slow_in, slow_in + 1)

    def env_copy(i):
        p = out_order[i]
        return pltpu.make_async_copy(
            env_ref.at[pl.ds(2 * p, 2)], env.at[pl.ds(2 * p, 2)], env_sem.at[i]
        )

    small_copies = (
        pltpu.make_async_copy(dims_hbm, dims_ref, small_sem.at[0]),
        pltpu.make_async_copy(energy_hbm, energy_ref, small_sem.at[1]),
    )
    for copy in small_copies:
        copy.start()
    for i in range(PAIRS):
        env_copy(i).start()
    own_start_copy = pltpu.make_async_copy(start_ref, own_start, start_sem)
    own_start_copy.start()

    barrier = pltpu.get_barrier_semaphore()
    for o in X_SIDES + Y_SIDES + Z_SIDES:
        pl.semaphore_signal(barrier, inc=1, device_id=peer(o), device_id_type=MESH)

    def pass_on(i):
        if i > 0:
            pl.semaphore_wait(gossip.at[i - 1], 2)
        if i < len(GOSSIP):
            for o in GOSSIP[i]:
                pl.semaphore_signal(
                    gossip.at[i], inc=1, device_id=peer(o), device_id_type=MESH
                )

    for copy in small_copies:
        copy.wait()

    kept = jnp.concatenate(
        [jnp.full((1, BS), dims_ref[0, j].astype(f32), f32) for j in range(NS)], axis=0
    )
    own_meta = jnp.concatenate([energy_ref[...].astype(f32), kept], axis=0)
    meta_out[...] = own_meta.astype(bf16)
    meta[0] = own_meta

    row = lax.broadcasted_iota(jnp.int32, (BS, BS), 0)
    col = lax.broadcasted_iota(jnp.int32, (BS, BS), 1)
    upper = row <= col
    on_diag = row == col

    diag_f[...] = jnp.zeros_like(diag_f)
    far_vec[...] = jnp.zeros_like(far_vec)
    vec[...] = jnp.zeros_like(vec)
    img[...] = jnp.zeros_like(img)
    state[...] = jnp.zeros_like(state)

    def grouped(lo, hi, fn):
        whole = (hi - lo) // GROUP

        def body(g, _):
            for j in range(GROUP):
                fn(lo + g * GROUP + j)
            return 0

        lax.fori_loop(0, whole, body, 0)
        for w in range(lo + whole * GROUP, hi):
            fn(w)

    def symmetrise(p, w):
        halves = []
        for q in range(2):
            u = 2 * p + q
            raw = env[u, w]
            whole = raw.astype(f32) + jnp.swapaxes(raw, 0, 1).astype(f32)
            env[u, w] = whole.astype(bf16)
            halves.append(whole)
            diag_f[u, pl.ds(w, 1), :] = jnp.sum(
                jnp.where(on_diag, whole, 0.0), axis=0, keepdims=True
            )
        packed[p, w] = jnp.where(upper, halves[0], halves[1]).astype(bf16)

    def pack_copy(p, c):
        lo, hi = SPLITS[c]
        target = jnp.where(p < 2, before[0], after[0])
        return pltpu.make_async_remote_copy(
            src_ref=packed.at[p, pl.ds(lo, hi - lo)],
            dst_ref=arrived.at[p, pl.ds(lo, hi - lo)],
            send_sem=pack_s.at[p, c], recv_sem=pack_r.at[p, c],
            device_id=(target, s), device_id_type=MESH,
        )

    def diag_copy(p):
        target = jnp.where(p < 2, before[0], after[0])
        return pltpu.make_async_remote_copy(
            src_ref=diag.at[pl.ds(2 * p, 2)], dst_ref=diag.at[pl.ds(NS + 2 * p, 2)],
            send_sem=diag_s.at[p], recv_sem=diag_r.at[p],
            device_id=(target, s), device_id_type=MESH,
        )

    meta_copies = [
        pltpu.make_async_remote_copy(
            src_ref=meta_out, dst_ref=meta_in.at[slot],
            send_sem=meta_s.at[slot], recv_sem=meta_r.at[slot],
            device_id=target, device_id_type=MESH,
        )
        for slot, target in ((0, before), (1, after))
    ]
    start_copy = pltpu.make_async_remote_copy(
        src_ref=start_ref.at[pl.ds(NS // 2, NS // 2)], dst_ref=far_start,
        send_sem=start_s, recv_sem=start_r, device_id=after, device_id_type=MESH,
    )

    for i in range(PAIRS):
        p = out_order[i]
        env_copy(i).wait()
        for c, (lo, hi) in enumerate(SPLITS):
            grouped(lo, hi, functools.partial(symmetrise, p))
            if i > 0 and c < len(SPLITS) - 1:
                pack_copy(p, c).start()
        for q in range(2):
            diag[2 * p + q] = diag_f[2 * p + q].astype(bf16)
        if i == 0:
            pl.semaphore_wait(barrier, 6)
            for copy in meta_copies:
                copy.start()
            start_copy.start()
            pack_copy(p, 0).start()
            pass_on(0)
        diag_copy(p).start()
        pack_copy(p, len(SPLITS) - 1).start()

    pass_on(1)
    own_start_copy.wait()

    def left_at(u):
        return jnp.where(u < 4, u, NS + u)

    def right_at(u):
        return jnp.where(u < 4, NS + u, u)

    def mask_of(row_seg, col_seg, u):
        rows_kept = meta[row_seg, pl.ds(NS + u, 1), :]
        cols_kept = meta[col_seg, pl.ds(NS + u, 1), :]
        live = (row.astype(f32) < rows_kept) & (col.astype(f32) < cols_kept)
        return live.astype(f32)

    def set_up(u, _):
        row_seg = jnp.where(u < 4, 0, 2)
        col_seg = jnp.where(u < 4, 1, 0)
        live = mask_of(row_seg, col_seg, u)
        mask[u] = live
        by_row = jnp.broadcast_to(meta[row_seg, pl.ds(u, 1), :], (BS, BS))
        energy[u] = jnp.swapaxes(by_row, 0, 1) + meta[col_seg, pl.ds(u, 1), :]
        return 0

    def open_here():
        meta_copies[0].wait_recv()
        meta[1] = meta_in[0].astype(f32)
        lax.fori_loop(0, 4, set_up, 0)
        for j in range(NS // 2):
            tri[j] = mask[j] * own_start[j].astype(f32)
            far_tri[0, j] = mask_of(0, 1, 4 + j) * own_start[4 + j].astype(f32)

    def open_before():
        meta_copies[1].wait_recv()
        meta[2] = meta_in[1].astype(f32)
        lax.fori_loop(4, 8, set_up, 0)
        start_copy.wait_recv()
        for j in range(NS // 2):
            tri[4 + j] = mask[4 + j] * far_start[j].astype(f32)

    def apply_env(x, u, lo, hi):
        n = hi - lo
        left = env[left_at(u), pl.ds(lo, n)].reshape(n * BS, BS)
        right = env[right_at(u), pl.ds(lo, n)].reshape(n * BS, BS)
        half = jnp.dot(left, x, preferred_element_type=f32).astype(bf16)
        half = half.reshape(n, BS, BS)
        half = jnp.concatenate([half[w] for w in range(n)], axis=1)
        return jnp.dot(half, right, preferred_element_type=f32)

    def unpack(p, w):
        sent = arrived[p, w]
        there = sent.astype(f32)
        back = jnp.swapaxes(sent, 0, 1).astype(f32)
        u = NS + 2 * p
        env[u, w] = jnp.where(upper, there, back).astype(bf16)
        second = jnp.where(upper, back, there)
        second = jnp.where(on_diag, far_diag_f[p, pl.ds(w, 1), :], second)
        env[u + 1, w] = second.astype(bf16)

    lane = lax.broadcasted_iota(jnp.int32, (1, BS), 1)
    pick = lax.broadcasted_iota(jnp.int32, (8, BS), 0) == lax.broadcasted_iota(
        jnp.int32, (8, BS), 1
    )
    nothing = jnp.zeros((8, BS), f32)

    def send_sums(chain, step, sums):
        other = jnp.where(chain == 0, seg_of[1], seg_of[-1])
        tile = [jnp.sum(x, axis=0, keepdims=True) for x in sums]
        tile += [jnp.zeros((8 - len(sums), BS), f32)]
        tile = jnp.sum(jnp.concatenate(tile, axis=0), axis=1, keepdims=True)
        line = jnp.sum(jnp.where(pick, tile, 0.0), axis=0, keepdims=True)
        part[chain, step] = line
        for o in FAR_FIRST:
            slot, seg = (1 - chain, other) if o[0] else (chain, k)
            pltpu.make_async_remote_copy(
                src_ref=part.at[chain, step], dst_ref=rows.at[slot, step, ROW[o]],
                send_sem=red_s.at[chain, step], recv_sem=red_r.at[slot, step],
                device_id=(seg, z_of[o[2]] + y_of[o[1]]), device_id_type=MESH,
            ).start()

    def open_chain(chain):
        def first_sums(u, sums):
            x = tri[u]
            return (sums[0] + fold(x * x), sums[1] + fold(x * tri_img[u]))

        norm, ray = lax.fori_loop(4 * chain, 4 * chain + 4, first_sums, (nothing,) * 2)
        send_sums(chain, 0, (nothing, norm, nothing, ray, nothing))

    for i in range(PAIRS):
        p = in_order[i]
        if i % 2 == 0:
            pl.when(p == 0)(open_here)
            pl.when(p == 2)(open_before)
        for c, (lo, hi) in enumerate(SPLITS):
            if c == 0:
                diag_copy(p).wait_recv()
                far_diag_f[p] = diag[NS + 2 * p + 1].astype(f32)
            pack_copy(p, c).wait_recv()
            grouped(lo, hi, functools.partial(unpack, p))
            at = i * len(SPLITS) + c + 2
            if at <= len(GOSSIP):
                pass_on(at)
            for q in range(2):
                u = 2 * p + q
                more = apply_env(tri[u].astype(bf16), u, lo, hi)
                if c == 0:
                    tri_img[u] = more
                else:
                    tri_img[u] = mask[u] * (tri_img[u] + more + energy[u] * tri[u])
            if c == len(SPLITS) - 1:
                for q in range(2):
                    u = 2 * p + q
                    both = lax.dot_general(
                        diag[left_at(u)], diag[right_at(u)],
                        (((0,), (0,)), ((), ())), preferred_element_type=f32,
                    )
                    diag_full[u] = both + energy[u]
        if i >= 2:
            open_chain(core if i == 2 else 1 - core)

    def coefs_of(chain, step):
        got = rows.at[chain, step]
        pltpu.make_async_copy(got, got, red_r.at[chain, step]).wait()
        total = (jnp.sum(rows[chain, step], axis=0) + part[chain, step]) / COUNT
        vt, tt, ti, th, vh = (
            jnp.broadcast_to(
                jnp.sum(jnp.where(lane == q, total, 0.0), axis=1, keepdims=True), (1, BS)
            )
            for q in range(5)
        )
        rayleigh = state[chain, pl.ds(0, 1), :]
        vec_sq = state[chain, pl.ds(1, 1), :]
        trial_sq = jnp.maximum(tt - vt * vt * (2.0 - vec_sq), 0.0)
        shrink = 1.0 / jnp.sqrt(trial_sq + NORM_FLOOR)
        cross = vh + ti
        coupling = (ti - vt * rayleigh) * shrink
        curvature = (th - vt * cross + vt * vt * rayleigh) * shrink * shrink
        cosine, sine = rotation(rayleigh, coupling, curvature)
        cosine = jnp.where(step == 0, 0.0, cosine)
        sine = jnp.where(step == 0, 1.0, sine)
        grow_tri = sine * shrink
        grow_vec = cosine - grow_tri * vt
        mixed = grow_vec * grow_tri
        new_rayleigh = (
            grow_vec * grow_vec * rayleigh + mixed * cross + grow_tri * grow_tri * th
        )
        state[chain, pl.ds(0, 1), :] = new_rayleigh
        state[chain, pl.ds(1, 1), :] = (
            grow_vec * grow_vec * vec_sq + 2.0 * mixed * vt + grow_tri * grow_tri * tt
        )
        return grow_vec, grow_tri, new_rayleigh

    def tri_copy(step, p):
        return pltpu.make_async_remote_copy(
            src_ref=tri.at[pl.ds(2 * p, 2)],
            dst_ref=far_tri.at[step + 1, pl.ds(2 * p - 4, 2)],
            send_sem=tri_s.at[step, p - 2], recv_sem=tri_r.at[step, p - 2],
            device_id=before, device_id_type=MESH,
        )

    def chain_step(chain, step):
        grow_vec, grow_tri, ray = coefs_of(chain, step)

        @pl.when((chain == 1) & (step >= 1))
        def _():
            for p in (2, 3):
                tri_copy(step - 1, p).wait_send()

        def advance(u):
            x = grow_vec * vec[u] + grow_tri * tri[u]
            h = grow_vec * img[u] + grow_tri * tri_img[u]
            vec[u] = x
            img[u] = h
            t = (h - ray * x) / jnp.maximum(jnp.abs(diag_full[u] - ray), 1.0)
            tri[u] = t
            return t

        def measure(u, t, sums):
            th = mask[u] * (apply_env(t.astype(bf16), u, 0, W) + energy[u] * t)
            tri_img[u] = th
            x, h = vec[u], img[u]
            return (
                sums[0] + fold(x * t), sums[1] + fold(t * t), sums[2] + fold(t * h),
                sums[3] + fold(t * th), sums[4] + fold(x * th),
            )

        def two_sectors(p, sums):
            trials = [advance(2 * p + q) for q in range(2)]

            @pl.when(chain == 1)
            def _():
                tri_copy(step, p).start()

            for q in range(2):
                sums = measure(2 * p + q, trials[q], sums)
            return sums

        sums = lax.fori_loop(2 * chain, 2 * chain + 2, two_sectors, (nothing,) * 5)
        send_sums(chain, step + 1, sums)

        @pl.when(chain == 0)
        def _():
            @pl.when(step >= 1)
            def _():
                for p in (2, 3):
                    tri_copy(step - 1, p).wait_recv()

            def follow(j, _):
                far_vec[j] = grow_vec * far_vec[j] + grow_tri * far_tri[step, j]
                return 0

            lax.fori_loop(0, NS // 2, follow, 0)

    def turn(n, _):
        step = lax.div(n, 2)
        chain = jnp.where(lax.rem(n, 2) == 0, core, 1 - core)
        chain_step(chain, step)
        return 0

    lax.fori_loop(0, 2 * ITERS, turn, 0)

    def close(n, _):
        chain = jnp.where(n == 0, core, 1 - core)
        grow_vec, grow_tri, _ = coefs_of(chain, ITERS)

        @pl.when(chain == 0)
        def _():
            for p in (2, 3):
                tri_copy(ITERS - 1, p).wait_recv()
            for j in range(NS // 2):
                out_ref[j] = (grow_vec * vec[j] + grow_tri * tri[j]).astype(bf16)
                out_ref[4 + j] = (
                    grow_vec * far_vec[j] + grow_tri * far_tri[ITERS, j]
                ).astype(bf16)

        return 0

    lax.fori_loop(0, 2, close, 0)

    for p in (2, 3):
        tri_copy(ITERS - 1, p).wait_send()
    start_copy.wait_send()
    for copy in meta_copies:
        copy.wait_send()
    for i in range(PAIRS):
        diag_copy(out_order[i]).wait_send()
        for c in range(len(SPLITS)):
            pack_copy(out_order[i], c).wait_send()
    for chain in range(2):
        for step in range(ITERS + 1):
            sent = rows.at[chain, step]
            pltpu.make_async_copy(sent, sent, red_s.at[chain, step]).wait()


def per_device(environment, block_energy, basis_dims, start_wave):
    block = (NS, BS, BS)
    half = (NS // 2, BS, BS)
    dma = pltpu.SemaphoreType.DMA
    splits = len(SPLITS)
    wave = pl.pallas_call(
        kernel,
        out_shape=jax.ShapeDtypeStruct(block, bf16),
        in_specs=[
            pl.BlockSpec(memory_space=pltpu.HBM),
            pl.BlockSpec(memory_space=pltpu.HBM),
            pl.BlockSpec(memory_space=pltpu.HBM),
            pl.BlockSpec(memory_space=pltpu.HBM),
        ],
        out_specs=pl.BlockSpec(memory_space=pltpu.VMEM),
        scratch_shapes=[
            pltpu.SMEM((1, NS), jnp.int32),
            pltpu.VMEM((NS, BS), bf16),
            pltpu.VMEM((2 * NS, W, BS, BS), bf16),
            pltpu.VMEM((PAIRS, W, BS, BS), bf16),
            pltpu.VMEM((PAIRS, W, BS, BS), bf16),
            pltpu.VMEM((NS, WP, BS), f32),
            pltpu.VMEM((2 * NS, WP, BS), bf16),
            pltpu.VMEM((PAIRS, WP, BS), f32),
            pltpu.VMEM(block, bf16),
            pltpu.VMEM(half, bf16),
            pltpu.VMEM((16, BS), bf16),
            pltpu.VMEM((2, 16, BS), bf16),
            pltpu.VMEM((3, 16, BS), f32),
            pltpu.VMEM(block, f32),
            pltpu.VMEM(block, f32),
            pltpu.VMEM(block, f32),
            pltpu.VMEM(block, f32),
            pltpu.VMEM(block, f32),
            pltpu.VMEM(block, f32),
            pltpu.VMEM(block, f32),
            pltpu.VMEM((2, ITERS + 1, 1, BS), f32),
            pltpu.VMEM((2, ITERS + 1, len(PEERS), 1, BS), f32),
            pltpu.VMEM((2, 8, BS), f32),
            pltpu.VMEM((ITERS + 1,) + half, f32),
            pltpu.VMEM(half, f32),
            pltpu.SemaphoreType.REGULAR((len(GOSSIP),)), dma((2,)),
            dma((PAIRS,)), dma, dma((2,)), dma((2,)), dma, dma,
            dma((PAIRS,)), dma((PAIRS,)),
            dma((PAIRS, splits)), dma((PAIRS, splits)),
            dma((ITERS, 2)), dma((ITERS, 2)),
            dma((2, ITERS + 1)), dma((2, ITERS + 1)),
        ],
        compiler_params=pltpu.CompilerParams(
            collective_id=0, has_side_effects=True, vmem_limit_bytes=63 * 2**20
        ),
    )(basis_dims, block_energy[0], environment[0], start_wave[0])
    return wave[None]


def solution(mesh):
    placed = (
        P("seg", "sec", None, None, None),
        P("seg", "sec", None),
        P("seg", "sec"),
        P("seg", "sec", None, None),
    )
    return jax.shard_map(
        per_device,
        mesh=mesh,
        in_specs=placed,
        out_specs=P("seg", "sec", None, None),
        check_vma=False,
    )
```

```python
import functools

import jax
import jax.numpy as jnp
from jax import lax
from jax.experimental import pallas as pl
from jax.experimental.pallas import tpu as pltpu
from jax.sharding import PartitionSpec as P

ITERS = 4
SEG, SEC, YS, ZS = 8, 32, 4, 8
NS, W, BS = 8, 17, 128
WP = 32
PAIRS = 4
SPLITS = ((0, 8), (8, 13), (13, 17))
GROUP = 4
NORM_FLOOR = 1e-06
COUNT = float(SEC * NS * BS * BS)
MESH = pl.DeviceIdType.MESH
f32, bf16 = jnp.float32, jnp.bfloat16


def hops(offset):
    a, b, c = offset
    return abs(a) + min(b, YS - b) + min(c, ZS - c)


PEERS = [
    (a, b, c)
    for a in (0, 1)
    for b in range(YS)
    for c in range(ZS)
    if (a, b, c) != (0, 0, 0)
]
X_SIDES, Y_SIDES, Z_SIDES = (
    ((-1, 0, 0), (1, 0, 0)),
    ((0, 1, 0), (0, YS - 1, 0)),
    ((0, 0, 1), (0, 0, ZS - 1)),
)
GOSSIP = (Z_SIDES, Z_SIDES, Z_SIDES, Y_SIDES, Y_SIDES, X_SIDES)
FAR_FIRST = sorted(PEERS, key=lambda o: -hops(o))
ROW = {}
for a_, base_ in ((1, 0), (0, SEC)):
    for i_, o_ in enumerate([o for o in PEERS if o[0] == a_]):
        ROW[o_] = base_ + i_


def fold(product):
    return jnp.sum(product.reshape(BS // 8, 8, BS), axis=0)


def rotation(rayleigh, coupling, curvature):
    half_gap = 0.5 * (rayleigh - curvature)
    radius = jnp.sqrt(half_gap * half_gap + coupling * coupling)
    ritz = 0.5 * (rayleigh + curvature) - radius
    first = coupling + curvature - ritz
    second = -(coupling + rayleigh - ritz)
    length = jnp.sqrt(first * first + second * second)
    return first / length, second / length


def kernel(
    dims_hbm, energy_hbm, env_ref, start_ref, out_ref,
    dims_ref, energy_ref, env, packed, arrived, diag_f, diag, far_diag_f, own_start, far_start,
    meta_out, meta_in, meta, vec, img, tri, tri_img, diag_full, energy, mask,
    part, rows, state, far_tri, far_vec,
    gossip, small_sem, env_sem, start_sem, meta_s, meta_r, start_s, start_r, diag_s, diag_r,
    pack_s, pack_r, tri_s, tri_r, red_s, red_r,
):
    k = lax.axis_index("seg")
    s = lax.axis_index("sec")
    z, y = lax.div(s, YS), lax.rem(s, YS)
    core = lax.rem(k, 2)
    seg_of = {a: lax.rem(k + a + SEG, SEG) for a in (-1, 0, 1)}
    y_of = [lax.rem(y + b, YS) for b in range(YS)]
    z_of = [lax.rem(z + c, ZS) * YS for c in range(ZS)]

    def peer(o):
        a, b, c = o
        return (seg_of[a], z_of[c] + y_of[b])

    before, after = (seg_of[-1], s), (seg_of[1], s)

    slow_out = 2 * core
    slow_in = 2 - 2 * core
    out_order = (slow_out, slow_out + 1, slow_in, slow_in + 1)
    in_order = (slow_out, slow_out + 1, slow_in, slow_in + 1)

    def env_copy(i):
        p = out_order[i]
        return pltpu.make_async_copy(
            env_ref.at[pl.ds(2 * p, 2)], env.at[pl.ds(2 * p, 2)], env_sem.at[i]
        )

    small_copies = (
        pltpu.make_async_copy(dims_hbm, dims_ref, small_sem.at[0]),
        pltpu.make_async_copy(energy_hbm, energy_ref, small_sem.at[1]),
    )
    for copy in small_copies:
        copy.start()
    for i in range(PAIRS):
        env_copy(i).start()
    own_start_copy = pltpu.make_async_copy(start_ref, own_start, start_sem)
    own_start_copy.start()

    barrier = pltpu.get_barrier_semaphore()
    for o in X_SIDES + Y_SIDES + Z_SIDES:
        pl.semaphore_signal(barrier, inc=1, device_id=peer(o), device_id_type=MESH)

    def pass_on(i):
        if i > 0:
            pl.semaphore_wait(gossip.at[i - 1], 2)
        if i < len(GOSSIP):
            for o in GOSSIP[i]:
                pl.semaphore_signal(
                    gossip.at[i], inc=1, device_id=peer(o), device_id_type=MESH
                )

    for copy in small_copies:
        copy.wait()

    kept = jnp.concatenate(
        [jnp.full((1, BS), dims_ref[0, j].astype(f32), f32) for j in range(NS)], axis=0
    )
    own_meta = jnp.concatenate([energy_ref[...].astype(f32), kept], axis=0)
    meta_out[...] = own_meta.astype(bf16)
    meta[0] = own_meta

    row = lax.broadcasted_iota(jnp.int32, (BS, BS), 0)
    col = lax.broadcasted_iota(jnp.int32, (BS, BS), 1)
    upper = row <= col
    on_diag = row == col

    diag_f[...] = jnp.zeros_like(diag_f)
    far_vec[...] = jnp.zeros_like(far_vec)
    vec[...] = jnp.zeros_like(vec)
    img[...] = jnp.zeros_like(img)
    state[...] = jnp.zeros_like(state)

    def grouped(lo, hi, fn):
        whole = (hi - lo) // GROUP

        def body(g, _):
            for j in range(GROUP):
                fn(lo + g * GROUP + j)
            return 0

        lax.fori_loop(0, whole, body, 0)
        for w in range(lo + whole * GROUP, hi):
            fn(w)

    def symmetrise(p, w):
        halves = []
        for q in range(2):
            u = 2 * p + q
            raw = env[u, w]
            whole = raw.astype(f32) + jnp.swapaxes(raw, 0, 1).astype(f32)
            env[u, w] = whole.astype(bf16)
            halves.append(whole)
            diag_f[u, pl.ds(w, 1), :] = jnp.sum(
                jnp.where(on_diag, whole, 0.0), axis=0, keepdims=True
            )
        packed[p, w] = jnp.where(upper, halves[0], halves[1]).astype(bf16)

    def pack_copy(p, c):
        lo, hi = SPLITS[c]
        target = jnp.where(p < 2, before[0], after[0])
        return pltpu.make_async_remote_copy(
            src_ref=packed.at[p, pl.ds(lo, hi - lo)],
            dst_ref=arrived.at[p, pl.ds(lo, hi - lo)],
            send_sem=pack_s.at[p, c], recv_sem=pack_r.at[p, c],
            device_id=(target, s), device_id_type=MESH,
        )

    def diag_copy(p):
        target = jnp.where(p < 2, before[0], after[0])
        return pltpu.make_async_remote_copy(
            src_ref=diag.at[pl.ds(2 * p, 2)], dst_ref=diag.at[pl.ds(NS + 2 * p, 2)],
            send_sem=diag_s.at[p], recv_sem=diag_r.at[p],
            device_id=(target, s), device_id_type=MESH,
        )

    meta_copies = [
        pltpu.make_async_remote_copy(
            src_ref=meta_out, dst_ref=meta_in.at[slot],
            send_sem=meta_s.at[slot], recv_sem=meta_r.at[slot],
            device_id=target, device_id_type=MESH,
        )
        for slot, target in ((0, before), (1, after))
    ]
    start_copy = pltpu.make_async_remote_copy(
        src_ref=start_ref.at[pl.ds(NS // 2, NS // 2)], dst_ref=far_start,
        send_sem=start_s, recv_sem=start_r, device_id=after, device_id_type=MESH,
    )

    for i in range(PAIRS):
        p = out_order[i]
        env_copy(i).wait()
        for c, (lo, hi) in enumerate(SPLITS):
            grouped(lo, hi, functools.partial(symmetrise, p))
            if i > 0 and c < len(SPLITS) - 1:
                pack_copy(p, c).start()
        for q in range(2):
            diag[2 * p + q] = diag_f[2 * p + q].astype(bf16)
        if i == 0:
            pl.semaphore_wait(barrier, 6)
            for copy in meta_copies:
                copy.start()
            start_copy.start()
            for c in range(len(SPLITS) - 1):
                pack_copy(p, c).start()
            pass_on(0)
        diag_copy(p).start()
        pack_copy(p, len(SPLITS) - 1).start()

    pass_on(1)
    own_start_copy.wait()

    def left_at(u):
        return jnp.where(u < 4, u, NS + u)

    def right_at(u):
        return jnp.where(u < 4, NS + u, u)

    def mask_of(row_seg, col_seg, u):
        rows_kept = meta[row_seg, pl.ds(NS + u, 1), :]
        cols_kept = meta[col_seg, pl.ds(NS + u, 1), :]
        live = (row.astype(f32) < rows_kept) & (col.astype(f32) < cols_kept)
        return live.astype(f32)

    def set_up(u, _):
        row_seg = jnp.where(u < 4, 0, 2)
        col_seg = jnp.where(u < 4, 1, 0)
        live = mask_of(row_seg, col_seg, u)
        mask[u] = live
        by_row = jnp.broadcast_to(meta[row_seg, pl.ds(u, 1), :], (BS, BS))
        energy[u] = jnp.swapaxes(by_row, 0, 1) + meta[col_seg, pl.ds(u, 1), :]
        return 0

    def open_here():
        meta_copies[0].wait_recv()
        meta[1] = meta_in[0].astype(f32)
        lax.fori_loop(0, 4, set_up, 0)
        for j in range(NS // 2):
            tri[j] = mask[j] * own_start[j].astype(f32)
            far_tri[0, j] = mask_of(0, 1, 4 + j) * own_start[4 + j].astype(f32)

    def open_before():
        meta_copies[1].wait_recv()
        meta[2] = meta_in[1].astype(f32)
        lax.fori_loop(4, 8, set_up, 0)
        start_copy.wait_recv()
        for j in range(NS // 2):
            tri[4 + j] = mask[4 + j] * far_start[j].astype(f32)

    def apply_env(x, u, lo, hi):
        n = hi - lo
        left = env[left_at(u), pl.ds(lo, n)].reshape(n * BS, BS)
        right = env[right_at(u), pl.ds(lo, n)].reshape(n * BS, BS)
        half = jnp.dot(left, x, preferred_element_type=f32).astype(bf16)
        half = half.reshape(n, BS, BS)
        half = jnp.concatenate([half[w] for w in range(n)], axis=1)
        return jnp.dot(half, right, preferred_element_type=f32)

    def apply_pair(x, y, u, lo, hi):
        n = hi - lo
        none = jnp.zeros_like(x)
        both = jnp.concatenate(
            [jnp.concatenate([x, none], axis=1), jnp.concatenate([none, y], axis=1)], axis=0
        )
        left = jnp.concatenate(
            [env[left_at(u + q), pl.ds(lo, n)].reshape(n * BS, BS) for q in range(2)], axis=1
        )
        half = jnp.dot(left, both, preferred_element_type=f32).astype(bf16)
        half = half.reshape(n, BS, 2 * BS)
        return [
            jnp.dot(
                jnp.concatenate([half[w, :, q * BS : (q + 1) * BS] for w in range(n)], axis=1),
                env[right_at(u + q), pl.ds(lo, n)].reshape(n * BS, BS),
                preferred_element_type=f32,
            )
            for q in range(2)
        ]

    def unpack(p, w):
        sent = arrived[p, w]
        there = sent.astype(f32)
        back = jnp.swapaxes(sent, 0, 1).astype(f32)
        u = NS + 2 * p
        env[u, w] = jnp.where(upper, there, back).astype(bf16)
        second = jnp.where(upper, back, there)
        second = jnp.where(on_diag, far_diag_f[p, pl.ds(w, 1), :], second)
        env[u + 1, w] = second.astype(bf16)

    lane = lax.broadcasted_iota(jnp.int32, (1, BS), 1)
    pick = lax.broadcasted_iota(jnp.int32, (8, BS), 0) == lax.broadcasted_iota(
        jnp.int32, (8, BS), 1
    )
    nothing = jnp.zeros((8, BS), f32)

    def send_sums(chain, step, sums):
        other = jnp.where(chain == 0, seg_of[1], seg_of[-1])
        tile = [jnp.sum(x, axis=0, keepdims=True) for x in sums]
        tile += [jnp.zeros((8 - len(sums), BS), f32)]
        tile = jnp.sum(jnp.concatenate(tile, axis=0), axis=1, keepdims=True)
        line = jnp.sum(jnp.where(pick, tile, 0.0), axis=0, keepdims=True)
        part[chain, step] = line
        for o in FAR_FIRST:
            slot, seg = (1 - chain, other) if o[0] else (chain, k)
            pltpu.make_async_remote_copy(
                src_ref=part.at[chain, step], dst_ref=rows.at[slot, step, ROW[o]],
                send_sem=red_s.at[chain, step], recv_sem=red_r.at[slot, step],
                device_id=(seg, z_of[o[2]] + y_of[o[1]]), device_id_type=MESH,
            ).start()

    def open_chain(chain):
        def first_sums(u, sums):
            x = tri[u]
            return (sums[0] + fold(x * x), sums[1] + fold(x * tri_img[u]))

        norm, ray = lax.fori_loop(4 * chain, 4 * chain + 4, first_sums, (nothing,) * 2)
        send_sums(chain, 0, (nothing, norm, nothing, ray, nothing))

    for i in range(PAIRS):
        p = in_order[i]
        if i % 2 == 0:
            pl.when(p == 0)(open_here)
            pl.when(p == 2)(open_before)
        for c, (lo, hi) in enumerate(SPLITS):
            if c == 0:
                diag_copy(p).wait_recv()
                far_diag_f[p] = diag[NS + 2 * p + 1].astype(f32)
            pack_copy(p, c).wait_recv()
            grouped(lo, hi, functools.partial(unpack, p))
            at = i * len(SPLITS) + c + 2
            if at <= len(GOSSIP):
                pass_on(at)
            for q in range(2):
                u = 2 * p + q
                more = apply_env(tri[u].astype(bf16), u, lo, hi)
                if c == 0:
                    tri_img[u] = more
                elif c < len(SPLITS) - 1:
                    tri_img[u] += more
                else:
                    tri_img[u] = mask[u] * (tri_img[u] + more + energy[u] * tri[u])
            if c == len(SPLITS) - 1:
                for q in range(2):
                    u = 2 * p + q
                    both = lax.dot_general(
                        diag[left_at(u)], diag[right_at(u)],
                        (((0,), (0,)), ((), ())), preferred_element_type=f32,
                    )
                    diag_full[u] = both + energy[u]
        if i >= 2:
            open_chain(core if i == 2 else 1 - core)

    def coefs_of(chain, step):
        got = rows.at[chain, step]
        pltpu.make_async_copy(got, got, red_r.at[chain, step]).wait()
        total = (jnp.sum(rows[chain, step], axis=0) + part[chain, step]) / COUNT
        vt, tt, ti, th, vh = (
            jnp.broadcast_to(
                jnp.sum(jnp.where(lane == q, total, 0.0), axis=1, keepdims=True), (1, BS)
            )
            for q in range(5)
        )
        rayleigh = state[chain, pl.ds(0, 1), :]
        vec_sq = state[chain, pl.ds(1, 1), :]
        trial_sq = jnp.maximum(tt - vt * vt * (2.0 - vec_sq), 0.0)
        shrink = 1.0 / jnp.sqrt(trial_sq + NORM_FLOOR)
        cross = vh + ti
        coupling = (ti - vt * rayleigh) * shrink
        curvature = (th - vt * cross + vt * vt * rayleigh) * shrink * shrink
        cosine, sine = rotation(rayleigh, coupling, curvature)
        cosine = jnp.where(step == 0, 0.0, cosine)
        sine = jnp.where(step == 0, 1.0, sine)
        grow_tri = sine * shrink
        grow_vec = cosine - grow_tri * vt
        mixed = grow_vec * grow_tri
        new_rayleigh = (
            grow_vec * grow_vec * rayleigh + mixed * cross + grow_tri * grow_tri * th
        )
        state[chain, pl.ds(0, 1), :] = new_rayleigh
        state[chain, pl.ds(1, 1), :] = (
            grow_vec * grow_vec * vec_sq + 2.0 * mixed * vt + grow_tri * grow_tri * tt
        )
        return grow_vec, grow_tri, new_rayleigh

    def tri_copy(step, p):
        return pltpu.make_async_remote_copy(
            src_ref=tri.at[pl.ds(2 * p, 2)],
            dst_ref=far_tri.at[step + 1, pl.ds(2 * p - 4, 2)],
            send_sem=tri_s.at[step, p - 2], recv_sem=tri_r.at[step, p - 2],
            device_id=before, device_id_type=MESH,
        )

    def chain_step(chain, step):
        grow_vec, grow_tri, ray = coefs_of(chain, step)

        @pl.when((chain == 1) & (step >= 1))
        def _():
            for p in (2, 3):
                tri_copy(step - 1, p).wait_send()

        def advance(u):
            x = grow_vec * vec[u] + grow_tri * tri[u]
            h = grow_vec * img[u] + grow_tri * tri_img[u]
            vec[u] = x
            img[u] = h
            t = (h - ray * x) / jnp.maximum(jnp.abs(diag_full[u] - ray), 1.0)
            tri[u] = t
            return t

        def measure(u, t, whole, sums):
            th = mask[u] * (whole + energy[u] * t)
            tri_img[u] = th
            x, h = vec[u], img[u]
            return (
                sums[0] + fold(x * t), sums[1] + fold(t * t), sums[2] + fold(t * h),
                sums[3] + fold(t * th), sums[4] + fold(x * th),
            )

        def two_sectors(p, sums):
            trials = [advance(2 * p + q) for q in range(2)]

            @pl.when(chain == 1)
            def _():
                tri_copy(step, p).start()

            halves = [t.astype(bf16) for t in trials]
            parts = [apply_pair(*halves, 2 * p, lo, hi) for lo, hi in ((0, 8), (8, W))]
            for q in range(2):
                whole = functools.reduce(jnp.add, [part[q] for part in parts])
                sums = measure(2 * p + q, trials[q], whole, sums)
            return sums

        sums = lax.fori_loop(2 * chain, 2 * chain + 2, two_sectors, (nothing,) * 5)
        send_sums(chain, step + 1, sums)

        @pl.when(chain == 0)
        def _():
            @pl.when(step >= 1)
            def _():
                for p in (2, 3):
                    tri_copy(step - 1, p).wait_recv()

            def follow(j, _):
                far_vec[j] = grow_vec * far_vec[j] + grow_tri * far_tri[step, j]
                return 0

            lax.fori_loop(0, NS // 2, follow, 0)

    def turn(n, _):
        step = lax.div(n, 2)
        chain = jnp.where(lax.rem(n, 2) == 0, core, 1 - core)
        chain_step(chain, step)
        return 0

    lax.fori_loop(0, 2 * ITERS, turn, 0)

    def close(n, _):
        chain = jnp.where(n == 0, core, 1 - core)
        grow_vec, grow_tri, _ = coefs_of(chain, ITERS)

        @pl.when(chain == 0)
        def _():
            for p in (2, 3):
                tri_copy(ITERS - 1, p).wait_recv()
            for j in range(NS // 2):
                out_ref[j] = (grow_vec * vec[j] + grow_tri * tri[j]).astype(bf16)
                out_ref[4 + j] = (
                    grow_vec * far_vec[j] + grow_tri * far_tri[ITERS, j]
                ).astype(bf16)

        return 0

    lax.fori_loop(0, 2, close, 0)

    for p in (2, 3):
        tri_copy(ITERS - 1, p).wait_send()
    start_copy.wait_send()
    for copy in meta_copies:
        copy.wait_send()
    for i in range(PAIRS):
        diag_copy(out_order[i]).wait_send()
        for c in range(len(SPLITS)):
            pack_copy(out_order[i], c).wait_send()
    for chain in range(2):
        for step in range(ITERS + 1):
            sent = rows.at[chain, step]
            pltpu.make_async_copy(sent, sent, red_s.at[chain, step]).wait()


def per_device(environment, block_energy, basis_dims, start_wave):
    block = (NS, BS, BS)
    half = (NS // 2, BS, BS)
    dma = pltpu.SemaphoreType.DMA
    splits = len(SPLITS)
    wave = pl.pallas_call(
        kernel,
        out_shape=jax.ShapeDtypeStruct(block, bf16),
        in_specs=[
            pl.BlockSpec(memory_space=pltpu.HBM),
            pl.BlockSpec(memory_space=pltpu.HBM),
            pl.BlockSpec(memory_space=pltpu.HBM),
            pl.BlockSpec(memory_space=pltpu.HBM),
        ],
        out_specs=pl.BlockSpec(memory_space=pltpu.VMEM),
        scratch_shapes=[
            pltpu.SMEM((1, NS), jnp.int32),
            pltpu.VMEM((NS, BS), bf16),
            pltpu.VMEM((2 * NS, W, BS, BS), bf16),
            pltpu.VMEM((PAIRS, W, BS, BS), bf16),
            pltpu.VMEM((PAIRS, W, BS, BS), bf16),
            pltpu.VMEM((NS, WP, BS), f32),
            pltpu.VMEM((2 * NS, WP, BS), bf16),
            pltpu.VMEM((PAIRS, WP, BS), f32),
            pltpu.VMEM(block, bf16),
            pltpu.VMEM(half, bf16),
            pltpu.VMEM((16, BS), bf16),
            pltpu.VMEM((2, 16, BS), bf16),
            pltpu.VMEM((3, 16, BS), f32),
            pltpu.VMEM(block, f32),
            pltpu.VMEM(block, f32),
            pltpu.VMEM(block, f32),
            pltpu.VMEM(block, f32),
            pltpu.VMEM(block, f32),
            pltpu.VMEM(block, f32),
            pltpu.VMEM(block, f32),
            pltpu.VMEM((2, ITERS + 1, 1, BS), f32),
            pltpu.VMEM((2, ITERS + 1, len(PEERS), 1, BS), f32),
            pltpu.VMEM((2, 8, BS), f32),
            pltpu.VMEM((ITERS + 1,) + half, f32),
            pltpu.VMEM(half, f32),
            pltpu.SemaphoreType.REGULAR((len(GOSSIP),)), dma((2,)),
            dma((PAIRS,)), dma, dma((2,)), dma((2,)), dma, dma,
            dma((PAIRS,)), dma((PAIRS,)),
            dma((PAIRS, splits)), dma((PAIRS, splits)),
            dma((ITERS, 2)), dma((ITERS, 2)),
            dma((2, ITERS + 1)), dma((2, ITERS + 1)),
        ],
        compiler_params=pltpu.CompilerParams(
            collective_id=0, has_side_effects=True, vmem_limit_bytes=48 * 2**20
        ),
    )(*(
        pltpu.with_memory_space_constraint(x, pltpu.HBM)
        for x in (basis_dims, block_energy[0], environment[0], start_wave[0])
    ))
    return wave[None]


def solution(mesh):
    placed = (
        P("seg", "sec", None, None, None),
        P("seg", "sec", None),
        P("seg", "sec"),
        P("seg", "sec", None, None),
    )
    return jax.shard_map(
        per_device,
        mesh=mesh,
        in_specs=placed,
        out_specs=P("seg", "sec", None, None),
        check_vma=False,
    )
```

```python
import functools

import jax
import jax.numpy as jnp
from jax import lax
from jax.experimental import pallas as pl
from jax.experimental.pallas import tpu as pltpu
from jax.sharding import PartitionSpec as P

ITERS = 4
SEG, SEC, YS, ZS = 8, 32, 4, 8
NS, W, BS = 8, 17, 128
WP = 32
PAIRS = 4
SPLITS = ((0, 8), (8, 13), (13, 17))
GROUP = 4
NORM_FLOOR = 1e-06
COUNT = float(SEC * NS * BS * BS)
MESH = pl.DeviceIdType.MESH
f32, bf16 = jnp.float32, jnp.bfloat16


def hops(offset):
    a, b, c = offset
    return abs(a) + min(b, YS - b) + min(c, ZS - c)


PEERS = [
    (a, b, c)
    for a in (0, 1)
    for b in range(YS)
    for c in range(ZS)
    if (a, b, c) != (0, 0, 0)
]
X_SIDES, Y_SIDES, Z_SIDES = (
    ((-1, 0, 0), (1, 0, 0)),
    ((0, 1, 0), (0, YS - 1, 0)),
    ((0, 0, 1), (0, 0, ZS - 1)),
)
GOSSIP = (Z_SIDES, Z_SIDES, Z_SIDES, Y_SIDES, Y_SIDES, X_SIDES)
FAR_FIRST = sorted(PEERS, key=lambda o: -hops(o))
ROW = {}
for a_, base_ in ((1, 0), (0, SEC)):
    for i_, o_ in enumerate([o for o in PEERS if o[0] == a_]):
        ROW[o_] = base_ + i_


def fold(product):
    return jnp.sum(product.reshape(BS // 8, 8, BS), axis=0)


def rotation(rayleigh, coupling, curvature):
    half_gap = 0.5 * (rayleigh - curvature)
    radius = jnp.sqrt(half_gap * half_gap + coupling * coupling)
    ritz = 0.5 * (rayleigh + curvature) - radius
    first = coupling + curvature - ritz
    second = -(coupling + rayleigh - ritz)
    length = jnp.sqrt(first * first + second * second)
    return first / length, second / length


def kernel(
    dims_hbm, energy_hbm, env_ref, start_ref, out_ref,
    dims_ref, energy_ref, env, packed, arrived, diag_f, diag, far_diag_f, own_start, far_start,
    meta_out, meta_in, meta, vec, img, tri, tri_img, diag_full, energy, mask,
    part, rows, state, far_tri, far_vec,
    gossip, small_sem, env_sem, start_sem, meta_s, meta_r, start_s, start_r, diag_s, diag_r,
    pack_s, pack_r, tri_s, tri_r, red_s, red_r,
):
    k = lax.axis_index("seg")
    s = lax.axis_index("sec")
    z, y = lax.div(s, YS), lax.rem(s, YS)
    core = lax.rem(k, 2)
    seg_of = {a: lax.rem(k + a + SEG, SEG) for a in (-1, 0, 1)}
    y_of = [lax.rem(y + b, YS) for b in range(YS)]
    z_of = [lax.rem(z + c, ZS) * YS for c in range(ZS)]

    def peer(o):
        a, b, c = o
        return (seg_of[a], z_of[c] + y_of[b])

    before, after = (seg_of[-1], s), (seg_of[1], s)

    slow_out = 2 * core
    slow_in = 2 - 2 * core
    out_order = (slow_out, slow_in, slow_out + 1, slow_in + 1)
    in_order = (slow_out, slow_in, slow_out + 1, slow_in + 1)

    def env_copy(i):
        p = out_order[i]
        return pltpu.make_async_copy(
            env_ref.at[pl.ds(2 * p, 2)], env.at[pl.ds(2 * p, 2)], env_sem.at[i]
        )

    small_copies = (
        pltpu.make_async_copy(dims_hbm, dims_ref, small_sem.at[0]),
        pltpu.make_async_copy(energy_hbm, energy_ref, small_sem.at[1]),
    )
    for copy in small_copies:
        copy.start()
    for i in range(PAIRS):
        env_copy(i).start()
    own_start_copy = pltpu.make_async_copy(start_ref, own_start, start_sem)
    own_start_copy.start()

    barrier = pltpu.get_barrier_semaphore()
    for o in X_SIDES + Y_SIDES + Z_SIDES:
        pl.semaphore_signal(barrier, inc=1, device_id=peer(o), device_id_type=MESH)

    def pass_on(i):
        if i > 0:
            pl.semaphore_wait(gossip.at[i - 1], 2)
        if i < len(GOSSIP):
            for o in GOSSIP[i]:
                pl.semaphore_signal(
                    gossip.at[i], inc=1, device_id=peer(o), device_id_type=MESH
                )

    for copy in small_copies:
        copy.wait()

    kept = jnp.concatenate(
        [jnp.full((1, BS), dims_ref[0, j].astype(f32), f32) for j in range(NS)], axis=0
    )
    own_meta = jnp.concatenate([energy_ref[...].astype(f32), kept], axis=0)
    meta_out[...] = own_meta.astype(bf16)
    meta[0] = own_meta

    row = lax.broadcasted_iota(jnp.int32, (BS, BS), 0)
    col = lax.broadcasted_iota(jnp.int32, (BS, BS), 1)
    upper = row <= col
    on_diag = row == col

    diag_f[...] = jnp.zeros_like(diag_f)
    far_vec[...] = jnp.zeros_like(far_vec)
    vec[...] = jnp.zeros_like(vec)
    img[...] = jnp.zeros_like(img)
    state[...] = jnp.zeros_like(state)

    def grouped(lo, hi, fn):
        whole = (hi - lo) // GROUP

        def body(g, _):
            for j in range(GROUP):
                fn(lo + g * GROUP + j)
            return 0

        lax.fori_loop(0, whole, body, 0)
        for w in range(lo + whole * GROUP, hi):
            fn(w)

    def symmetrise(p, w):
        halves = []
        for q in range(2):
            u = 2 * p + q
            raw = env[u, w]
            whole = raw.astype(f32) + jnp.swapaxes(raw, 0, 1).astype(f32)
            env[u, w] = whole.astype(bf16)
            halves.append(whole)
            diag_f[u, pl.ds(w, 1), :] = jnp.sum(
                jnp.where(on_diag, whole, 0.0), axis=0, keepdims=True
            )
        packed[p, w] = jnp.where(upper, halves[0], halves[1]).astype(bf16)

    def pack_copy(p, c):
        lo, hi = SPLITS[c]
        target = jnp.where(p < 2, before[0], after[0])
        return pltpu.make_async_remote_copy(
            src_ref=packed.at[p, pl.ds(lo, hi - lo)],
            dst_ref=arrived.at[p, pl.ds(lo, hi - lo)],
            send_sem=pack_s.at[p, c], recv_sem=pack_r.at[p, c],
            device_id=(target, s), device_id_type=MESH,
        )

    def diag_copy(p):
        target = jnp.where(p < 2, before[0], after[0])
        return pltpu.make_async_remote_copy(
            src_ref=diag.at[pl.ds(2 * p, 2)], dst_ref=diag.at[pl.ds(NS + 2 * p, 2)],
            send_sem=diag_s.at[p], recv_sem=diag_r.at[p],
            device_id=(target, s), device_id_type=MESH,
        )

    meta_copies = [
        pltpu.make_async_remote_copy(
            src_ref=meta_out, dst_ref=meta_in.at[slot],
            send_sem=meta_s.at[slot], recv_sem=meta_r.at[slot],
            device_id=target, device_id_type=MESH,
        )
        for slot, target in ((0, before), (1, after))
    ]
    start_copy = pltpu.make_async_remote_copy(
        src_ref=start_ref.at[pl.ds(NS // 2, NS // 2)], dst_ref=far_start,
        send_sem=start_s, recv_sem=start_r, device_id=after, device_id_type=MESH,
    )

    for i in range(PAIRS):
        p = out_order[i]
        env_copy(i).wait()
        for c, (lo, hi) in enumerate(SPLITS):
            grouped(lo, hi, functools.partial(symmetrise, p))
            if i > 0 and c < len(SPLITS) - 1:
                pack_copy(p, c).start()
        for q in range(2):
            diag[2 * p + q] = diag_f[2 * p + q].astype(bf16)
        if i == 0:
            pl.semaphore_wait(barrier, 6)
            for copy in meta_copies:
                copy.start()
            start_copy.start()
            for c in range(len(SPLITS) - 1):
                pack_copy(p, c).start()
            pass_on(0)
        diag_copy(p).start()
        pack_copy(p, len(SPLITS) - 1).start()

    pass_on(1)
    own_start_copy.wait()

    def left_at(u):
        return jnp.where(u < 4, u, NS + u)

    def right_at(u):
        return jnp.where(u < 4, NS + u, u)

    def mask_of(row_seg, col_seg, u):
        rows_kept = meta[row_seg, pl.ds(NS + u, 1), :]
        cols_kept = meta[col_seg, pl.ds(NS + u, 1), :]
        live = (row.astype(f32) < rows_kept) & (col.astype(f32) < cols_kept)
        return live.astype(f32)

    def set_up(u, _):
        row_seg = jnp.where(u < 4, 0, 2)
        col_seg = jnp.where(u < 4, 1, 0)
        live = mask_of(row_seg, col_seg, u)
        mask[u] = live
        by_row = jnp.broadcast_to(meta[row_seg, pl.ds(u, 1), :], (BS, BS))
        energy[u] = jnp.swapaxes(by_row, 0, 1) + meta[col_seg, pl.ds(u, 1), :]
        return 0

    def open_here():
        meta_copies[0].wait_recv()
        meta[1] = meta_in[0].astype(f32)
        lax.fori_loop(0, 4, set_up, 0)
        for j in range(NS // 2):
            tri[j] = mask[j] * own_start[j].astype(f32)
            far_tri[0, j] = mask_of(0, 1, 4 + j) * own_start[4 + j].astype(f32)

    def open_before():
        meta_copies[1].wait_recv()
        meta[2] = meta_in[1].astype(f32)
        lax.fori_loop(4, 8, set_up, 0)
        start_copy.wait_recv()
        for j in range(NS // 2):
            tri[4 + j] = mask[4 + j] * far_start[j].astype(f32)

    def apply_env(x, u, lo, hi):
        n = hi - lo
        left = env[left_at(u), pl.ds(lo, n)].reshape(n * BS, BS)
        right = env[right_at(u), pl.ds(lo, n)].reshape(n * BS, BS)
        half = jnp.dot(left, x, preferred_element_type=f32).astype(bf16)
        half = half.reshape(n, BS, BS)
        half = jnp.concatenate([half[w] for w in range(n)], axis=1)
        return jnp.dot(half, right, preferred_element_type=f32)

    def apply_pair(x, y, u, lo, hi):
        n = hi - lo
        none = jnp.zeros_like(x)
        both = jnp.concatenate(
            [jnp.concatenate([x, none], axis=1), jnp.concatenate([none, y], axis=1)], axis=0
        )
        left = jnp.concatenate(
            [env[left_at(u + q), pl.ds(lo, n)].reshape(n * BS, BS) for q in range(2)], axis=1
        )
        half = jnp.dot(left, both, preferred_element_type=f32).astype(bf16)
        half = half.reshape(n, BS, 2 * BS)
        return [
            jnp.dot(
                jnp.concatenate([half[w, :, q * BS : (q + 1) * BS] for w in range(n)], axis=1),
                env[right_at(u + q), pl.ds(lo, n)].reshape(n * BS, BS),
                preferred_element_type=f32,
            )
            for q in range(2)
        ]

    def unpack(p, w):
        sent = arrived[p, w]
        there = sent.astype(f32)
        back = jnp.swapaxes(sent, 0, 1).astype(f32)
        u = NS + 2 * p
        env[u, w] = jnp.where(upper, there, back).astype(bf16)
        second = jnp.where(upper, back, there)
        second = jnp.where(on_diag, far_diag_f[p, pl.ds(w, 1), :], second)
        env[u + 1, w] = second.astype(bf16)

    lane = lax.broadcasted_iota(jnp.int32, (1, BS), 1)
    pick = lax.broadcasted_iota(jnp.int32, (8, BS), 0) == lax.broadcasted_iota(
        jnp.int32, (8, BS), 1
    )
    nothing = jnp.zeros((8, BS), f32)

    def send_sums(chain, step, sums):
        other = jnp.where(chain == 0, seg_of[1], seg_of[-1])
        tile = [jnp.sum(x, axis=0, keepdims=True) for x in sums]
        tile += [jnp.zeros((8 - len(sums), BS), f32)]
        tile = jnp.sum(jnp.concatenate(tile, axis=0), axis=1, keepdims=True)
        line = jnp.sum(jnp.where(pick, tile, 0.0), axis=0, keepdims=True)
        part[chain, step] = line
        for o in FAR_FIRST:
            slot, seg = (1 - chain, other) if o[0] else (chain, k)
            pltpu.make_async_remote_copy(
                src_ref=part.at[chain, step], dst_ref=rows.at[slot, step, ROW[o]],
                send_sem=red_s.at[chain, step], recv_sem=red_r.at[slot, step],
                device_id=(seg, z_of[o[2]] + y_of[o[1]]), device_id_type=MESH,
            ).start()

    def open_chain(chain):
        def first_sums(u, sums):
            x = tri[u]
            return (sums[0] + fold(x * x), sums[1] + fold(x * tri_img[u]))

        norm, ray = lax.fori_loop(4 * chain, 4 * chain + 4, first_sums, (nothing,) * 2)
        send_sums(chain, 0, (nothing, norm, nothing, ray, nothing))

    for i in range(PAIRS):
        p = in_order[i]
        if i < 2:
            pl.when(p == 0)(open_here)
            pl.when(p == 2)(open_before)
        for c, (lo, hi) in enumerate(SPLITS):
            if c == 0:
                diag_copy(p).wait_recv()
                far_diag_f[p] = diag[NS + 2 * p + 1].astype(f32)
            pack_copy(p, c).wait_recv()
            grouped(lo, hi, functools.partial(unpack, p))
            at = i * len(SPLITS) + c + 2
            if at <= len(GOSSIP):
                pass_on(at)
            for q in range(2):
                u = 2 * p + q
                more = apply_env(tri[u].astype(bf16), u, lo, hi)
                if c == 0:
                    tri_img[u] = more
                elif c < len(SPLITS) - 1:
                    tri_img[u] += more
                else:
                    tri_img[u] = mask[u] * (tri_img[u] + more + energy[u] * tri[u])
            if c == len(SPLITS) - 1:
                for q in range(2):
                    u = 2 * p + q
                    both = lax.dot_general(
                        diag[left_at(u)], diag[right_at(u)],
                        (((0,), (0,)), ((), ())), preferred_element_type=f32,
                    )
                    diag_full[u] = both + energy[u]
        if i >= 2:
            open_chain(core if i == 2 else 1 - core)

    def coefs_of(chain, step):
        got = rows.at[chain, step]
        pltpu.make_async_copy(got, got, red_r.at[chain, step]).wait()
        total = (jnp.sum(rows[chain, step], axis=0) + part[chain, step]) / COUNT
        vt, tt, ti, th, vh = (
            jnp.broadcast_to(
                jnp.sum(jnp.where(lane == q, total, 0.0), axis=1, keepdims=True), (1, BS)
            )
            for q in range(5)
        )
        rayleigh = state[chain, pl.ds(0, 1), :]
        vec_sq = state[chain, pl.ds(1, 1), :]
        trial_sq = jnp.maximum(tt - vt * vt * (2.0 - vec_sq), 0.0)
        shrink = 1.0 / jnp.sqrt(trial_sq + NORM_FLOOR)
        cross = vh + ti
        coupling = (ti - vt * rayleigh) * shrink
        curvature = (th - vt * cross + vt * vt * rayleigh) * shrink * shrink
        cosine, sine = rotation(rayleigh, coupling, curvature)
        cosine = jnp.where(step == 0, 0.0, cosine)
        sine = jnp.where(step == 0, 1.0, sine)
        grow_tri = sine * shrink
        grow_vec = cosine - grow_tri * vt
        mixed = grow_vec * grow_tri
        new_rayleigh = (
            grow_vec * grow_vec * rayleigh + mixed * cross + grow_tri * grow_tri * th
        )
        state[chain, pl.ds(0, 1), :] = new_rayleigh
        state[chain, pl.ds(1, 1), :] = (
            grow_vec * grow_vec * vec_sq + 2.0 * mixed * vt + grow_tri * grow_tri * tt
        )
        return grow_vec, grow_tri, new_rayleigh

    def tri_copy(step, p):
        return pltpu.make_async_remote_copy(
            src_ref=tri.at[pl.ds(2 * p, 2)],
            dst_ref=far_tri.at[step + 1, pl.ds(2 * p - 4, 2)],
            send_sem=tri_s.at[step, p - 2], recv_sem=tri_r.at[step, p - 2],
            device_id=before, device_id_type=MESH,
        )

    def chain_step(chain, step):
        grow_vec, grow_tri, ray = coefs_of(chain, step)

        @pl.when((chain == 1) & (step >= 1))
        def _():
            for p in (2, 3):
                tri_copy(step - 1, p).wait_send()

        def advance(u):
            x = grow_vec * vec[u] + grow_tri * tri[u]
            h = grow_vec * img[u] + grow_tri * tri_img[u]
            vec[u] = x
            img[u] = h
            t = (h - ray * x) / jnp.maximum(jnp.abs(diag_full[u] - ray), 1.0)
            tri[u] = t
            return t

        def measure(u, t, whole, sums):
            th = mask[u] * (whole + energy[u] * t)
            tri_img[u] = th
            x, h = vec[u], img[u]
            return (
                sums[0] + fold(x * t), sums[1] + fold(t * t), sums[2] + fold(t * h),
                sums[3] + fold(t * th), sums[4] + fold(x * th),
            )

        def two_sectors(p, sums):
            trials = [advance(2 * p + q) for q in range(2)]

            @pl.when(chain == 1)
            def _():
                tri_copy(step, p).start()

            halves = [t.astype(bf16) for t in trials]
            parts = [apply_pair(*halves, 2 * p, lo, hi) for lo, hi in ((0, 8), (8, W))]
            for q in range(2):
                whole = functools.reduce(jnp.add, [part[q] for part in parts])
                sums = measure(2 * p + q, trials[q], whole, sums)
            return sums

        sums = lax.fori_loop(2 * chain, 2 * chain + 2, two_sectors, (nothing,) * 5)
        send_sums(chain, step + 1, sums)

        @pl.when(chain == 0)
        def _():
            @pl.when(step >= 1)
            def _():
                for p in (2, 3):
                    tri_copy(step - 1, p).wait_recv()

            def follow(j, _):
                far_vec[j] = grow_vec * far_vec[j] + grow_tri * far_tri[step, j]
                return 0

            lax.fori_loop(0, NS // 2, follow, 0)

    def turn(n, _):
        step = lax.div(n, 2)
        chain = jnp.where(lax.rem(n, 2) == 0, core, 1 - core)
        chain_step(chain, step)
        return 0

    lax.fori_loop(0, 2 * ITERS, turn, 0)

    def close(n, _):
        chain = jnp.where(n == 0, core, 1 - core)
        grow_vec, grow_tri, _ = coefs_of(chain, ITERS)

        @pl.when(chain == 0)
        def _():
            for p in (2, 3):
                tri_copy(ITERS - 1, p).wait_recv()
            for j in range(NS // 2):
                out_ref[j] = (grow_vec * vec[j] + grow_tri * tri[j]).astype(bf16)
                out_ref[4 + j] = (
                    grow_vec * far_vec[j] + grow_tri * far_tri[ITERS, j]
                ).astype(bf16)

        return 0

    lax.fori_loop(0, 2, close, 0)

    for p in (2, 3):
        tri_copy(ITERS - 1, p).wait_send()
    start_copy.wait_send()
    for copy in meta_copies:
        copy.wait_send()
    for i in range(PAIRS):
        diag_copy(out_order[i]).wait_send()
        for c in range(len(SPLITS)):
            pack_copy(out_order[i], c).wait_send()
    for chain in range(2):
        for step in range(ITERS + 1):
            sent = rows.at[chain, step]
            pltpu.make_async_copy(sent, sent, red_s.at[chain, step]).wait()


def per_device(environment, block_energy, basis_dims, start_wave):
    block = (NS, BS, BS)
    half = (NS // 2, BS, BS)
    dma = pltpu.SemaphoreType.DMA
    splits = len(SPLITS)
    wave = pl.pallas_call(
        kernel,
        out_shape=jax.ShapeDtypeStruct(block, bf16),
        in_specs=[
            pl.BlockSpec(memory_space=pltpu.HBM),
            pl.BlockSpec(memory_space=pltpu.HBM),
            pl.BlockSpec(memory_space=pltpu.HBM),
            pl.BlockSpec(memory_space=pltpu.HBM),
        ],
        out_specs=pl.BlockSpec(memory_space=pltpu.VMEM),
        scratch_shapes=[
            pltpu.SMEM((1, NS), jnp.int32),
            pltpu.VMEM((NS, BS), bf16),
            pltpu.VMEM((2 * NS, W, BS, BS), bf16),
            pltpu.VMEM((PAIRS, W, BS, BS), bf16),
            pltpu.VMEM((PAIRS, W, BS, BS), bf16),
            pltpu.VMEM((NS, WP, BS), f32),
            pltpu.VMEM((2 * NS, WP, BS), bf16),
            pltpu.VMEM((PAIRS, WP, BS), f32),
            pltpu.VMEM(block, bf16),
            pltpu.VMEM(half, bf16),
            pltpu.VMEM((16, BS), bf16),
            pltpu.VMEM((2, 16, BS), bf16),
            pltpu.VMEM((3, 16, BS), f32),
            pltpu.VMEM(block, f32),
            pltpu.VMEM(block, f32),
            pltpu.VMEM(block, f32),
            pltpu.VMEM(block, f32),
            pltpu.VMEM(block, f32),
            pltpu.VMEM(block, f32),
            pltpu.VMEM(block, f32),
            pltpu.VMEM((2, ITERS + 1, 1, BS), f32),
            pltpu.VMEM((2, ITERS + 1, len(PEERS), 1, BS), f32),
            pltpu.VMEM((2, 8, BS), f32),
            pltpu.VMEM((ITERS + 1,) + half, f32),
            pltpu.VMEM(half, f32),
            pltpu.SemaphoreType.REGULAR((len(GOSSIP),)), dma((2,)),
            dma((PAIRS,)), dma, dma((2,)), dma((2,)), dma, dma,
            dma((PAIRS,)), dma((PAIRS,)),
            dma((PAIRS, splits)), dma((PAIRS, splits)),
            dma((ITERS, 2)), dma((ITERS, 2)),
            dma((2, ITERS + 1)), dma((2, ITERS + 1)),
        ],
        compiler_params=pltpu.CompilerParams(
            collective_id=0, has_side_effects=True, vmem_limit_bytes=48 * 2**20
        ),
    )(*(
        pltpu.with_memory_space_constraint(x, pltpu.HBM)
        for x in (basis_dims, block_energy[0], environment[0], start_wave[0])
    ))
    return wave[None]


def solution(mesh):
    placed = (
        P("seg", "sec", None, None, None),
        P("seg", "sec", None),
        P("seg", "sec"),
        P("seg", "sec", None, None),
    )
    return jax.shard_map(
        per_device,
        mesh=mesh,
        in_specs=placed,
        out_specs=P("seg", "sec", None, None),
        check_vma=False,
    )
```
